512 devices in a mesh: op: 8 (over z), sec: 64 (over x, y, core).
Axes of the slice: x: 4, y: 8, z: 8, core: 2. Of those that a mesh axis runs over, the one named last changes fastest.
Arguments:
- psi_first: bfloat16 [768, 128, 128], P('sec'), may hold values from -6 to 6
- psi_second: bfloat16 [768, 128, 128], P('sec'), may hold values from -6 to 6
- left_env: bfloat16 [40, 128, 128, 128], P('op', 'sec'), may hold values from -0.078125 to 0.078125
- right_env: bfloat16 [40, 6, 128, 128], P('op'), may hold values from -0.5 to 0.5
- links: int32 [8, 768], P('op'), may hold values from 0 to 767, as said below
Outputs:
- applied_first: bfloat16 [768, 128, 128], P('sec')
- applied_second: bfloat16 [768, 128, 128], P('sec')
The draws below stay inside these ranges and needn't reach their ends.
Inputs may be any that keep to these rules, and one draw needn't show every extreme that they name: Within each block of links formed by one index of op and one index of sec (8 // 8 groups by 12 tiles), at most 1 entries name tiles held by any one index of sec, and exactly 1 entries name tiles of some one index.
All inputs are finite; a program needn't handle non-finite values.
Results may differ from the reference program's by a relative error of at most 0.0049.
Values may be sent and summed in bfloat16 or wider, within the bound.
No kernel may reach another device: no remote copies, remote signals or barrier semaphores. Data moves between devices by JAX's collectives and lax.ppermute only.
A program may use at most 64 MiB of HBM per device.

```python
import jax
import jax.numpy as jnp
from jax import lax

B = 128
W = 40
TG = 5
NR = 6
TPD = 12
NA = 128
NT = 768
N_OP = 8
N_SEC = 64


def draw_links(key, part):
    key = jax.random.fold_in(key, 7)
    group_local = W // TG // N_OP
    entry_count = group_local * TPD
    capacity = max(1, (entry_count + N_SEC - 1) // N_SEC)

    def one_block(block_key):
        key_first, key_rest, key_order, key_local = jax.random.split(block_key, 4)
        busiest = jax.random.randint(key_first, (), 0, N_SEC)
        others = jax.random.permutation(key_rest, (N_SEC - 1) * capacity)[:entry_count - capacity] // capacity + 1
        owners = jnp.concatenate([jnp.zeros((capacity,), jnp.int32), others.astype(jnp.int32)])
        owners = (owners + busiest) % N_SEC
        owners = jax.random.permutation(key_order, owners)
        local_tile = jax.random.randint(key_local, (entry_count,), 0, TPD)
        return (owners * TPD + local_tile).reshape(group_local, TPD)
    block_keys = jax.random.split(key, N_OP * N_SEC)
    blocks = jax.vmap(one_block)(block_keys).reshape(N_OP, N_SEC, group_local, TPD)
    return blocks.transpose(0, 2, 1, 3).reshape(W // TG, N_SEC * TPD).astype(jnp.int32)


def steps_of(stream_key, dims, pieces, low, largest):
    gain, own = 1.0, jax.random.fold_in(stream_key, 6)
    for position, blocks in pieces:
        draws = jnp.exp(jax.random.uniform(jax.random.fold_in(own, position), (blocks,), jnp.float32, low / len(pieces), largest / len(pieces)))
        gain = gain * jnp.repeat(draws, dims[position] // blocks).reshape([-1 if axis == position else 1 for axis in range(len(dims))])
    return gain


def normal_values(key, dims, scale, reach, cuts=(), held_as=jnp.bfloat16):
    result = scale * jax.random.normal(key, dims, jnp.float32)
    if cuts:
        result = result * steps_of(key, dims, cuts, -0.22, 0.18)
    return jnp.clip(result, -reach, reach).astype(held_as)


def setup_inputs(seed: int = 0) -> dict:
    key_list = jax.random.split(jax.random.key(seed), 6)
    psi_first = normal_values(key_list[0], (NT, B, B), 1.0, 6.0, ((0, 64),))
    psi_second = normal_values(key_list[1], (NT, B, B), 1.0, 6.0, ((0, 64),))
    left_env = normal_values(key_list[2], (W, NA, B, B), (B * W) ** -0.5, 0.078125, ((0, 8), (1, 64)))
    right_env = normal_values(key_list[3], (W, NR, B, B), B ** -0.5, 0.5, ((0, 8),))
    links = draw_links(jax.random.fold_in(key_list[5], 71), 0)
    return {"psi_first": psi_first, "psi_second": psi_second, "left_env": left_env, "right_env": right_env, "links": links}


def reference(psi_first, psi_second, left_env, right_env, links):
    def add_term(current, term):
        group_index = term // TG
        source_ids = lax.dynamic_index_in_dim(links, group_index, 0, False)
        left_block = lax.dynamic_index_in_dim(left_env, term, 0, False).astype(jnp.float32)
        right_block = lax.dynamic_index_in_dim(right_env, term, 0, False).astype(jnp.float32)
        updated = []
        for vector, partial_sum in zip((psi_first, psi_second), current):
            source_grid = vector[source_ids].astype(jnp.float32).reshape(NA, NR, B, B)
            half_product = jnp.einsum("aij,anjk->anik", left_block, source_grid)
            half_product = lax.optimization_barrier(half_product.astype(jnp.bfloat16)).astype(jnp.float32)
            contracted = jnp.einsum("anik,nkl->anil", half_product, right_block)
            updated.append(partial_sum + contracted.reshape(NT, B, B))
        return (updated[0], updated[1]), None

    zeros_tiles = jnp.zeros((NT, B, B), jnp.float32)
    totals, unused = lax.scan(add_term, (zeros_tiles, zeros_tiles), jnp.arange(W, dtype=jnp.int32))
    return (totals[0].astype(jnp.bfloat16), totals[1].astype(jnp.bfloat16))
```

```python
import jax
import jax.numpy as jnp
import numpy as np
from jax import lax
from jax.experimental import pallas as pl
from jax.experimental.pallas import tpu as pltpu
from jax.sharding import Mesh, PartitionSpec as P

VMEM_LIMIT = 40 * 1024 * 1024
SLAB = 16


def dot(a, b):
    return jnp.dot(a, b, preferred_element_type=jnp.float32)


def swap_order(outer, inner):
    count = outer * inner
    matrix = np.zeros((count, count), np.float32)
    for o in range(outer):
        for i in range(inner):
            matrix[i * outer + o, o * inner + i] = 1
    return jnp.asarray(matrix, jnp.bfloat16)


def pick_parity(count):
    matrix = np.zeros((2, count, 2 * count), np.float32)
    for r in range(count):
        matrix[0, r, 2 * r] = 1
        matrix[1, r, 2 * r + 1] = 1
    return jnp.asarray(matrix, jnp.bfloat16)


def cut_kernel(which_ref, first_ref, second_ref, order_ref, out_ref):
    tiles, width, _ = first_ref.shape
    half = width // 2
    second = which_ref[0] == 1
    rows = 2 * tiles * SLAB
    for slab in range(half // SLAB):
        parts = []
        for k in range(tiles):
            for top in range(2):
                cut = slice(top * half + slab * SLAB, top * half + (slab + 1) * SLAB)
                parts.append(jnp.where(second, second_ref[k, cut, :], first_ref[k, cut, :]))
        block = dot(order_ref[...], jnp.concatenate(parts, axis=0))
        out_ref[slab * rows : (slab + 1) * rows, :] = block.astype(jnp.bfloat16)


def choose_kernel(pieces_ref, hot_ref, parity_ref, out_ref, wide):
    count = parity_ref.shape[1]
    lanes = pieces_ref.shape[1]
    for b in range(pieces_ref.shape[0] // (2 * count)):
        block = pieces_ref[2 * count * b : 2 * count * (b + 1), :]
        for top in range(2):
            picked = dot(parity_ref[top], block).astype(jnp.bfloat16)
            wide[count * b : count * (b + 1), top * lanes : (top + 1) * lanes] = picked
    step = 256
    for m in range(hot_ref.shape[0] // step):
        out_ref[m * step : (m + 1) * step, :] = dot(
            hot_ref[m * step : (m + 1) * step, :], wide[...]
        ).astype(jnp.bfloat16)


def apply_kernel(arrived_ref, left_a, left_b, right_a, right_b, order_ref, out_ref, tiles, halves):
    terms, lefts, width, _ = left_a.shape
    rights = right_a.shape[1]
    half = width // 2
    units = 2 * lefts * rights
    rows = units * SLAB
    for slab in range(half // SLAB):
        block = dot(order_ref[...], arrived_ref[slab * rows : (slab + 1) * rows, :])
        block = block.astype(jnp.bfloat16)
        for u in range(units):
            g, a, r = u // (lefts * rights), u // rights % lefts, u % rights
            for top in range(2):
                tiles[
                    g,
                    a,
                    top * half + slab * SLAB : top * half + (slab + 1) * SLAB,
                    r * width : (r + 1) * width,
                ] = block[u * SLAB : (u + 1) * SLAB, top * width : (top + 1) * width]
    for g, left in enumerate((left_a, left_b)):
        for a in range(lefts):
            stacked = jnp.concatenate([left[t, a] for t in range(terms)], axis=0)
            product = dot(stacked, tiles[g, a]).astype(jnp.bfloat16)
            for t in range(terms):
                for r in range(rights):
                    column = (g * terms + t) * width
                    halves[r, a * width : (a + 1) * width, column : column + width] = product[
                        t * width : (t + 1) * width, r * width : (r + 1) * width
                    ]
    for r in range(rights):
        stacked = jnp.concatenate(
            [right[t, r] for right in (right_a, right_b) for t in range(terms)], axis=0
        )
        total = dot(halves[r], stacked).astype(jnp.bfloat16)
        for a in range(lefts):
            out_ref[a * rights + r] = total[a * width : (a + 1) * width]


def call(kernel, shape, scratch=(), prefetch=0, name=None, operands=(), flops=0):
    vmem = pl.BlockSpec(memory_space=pltpu.VMEM)
    smem = pl.BlockSpec(memory_space=pltpu.SMEM)
    return pl.pallas_call(
        kernel,
        out_shape=jax.ShapeDtypeStruct(shape, jnp.bfloat16),
        in_specs=[smem] * prefetch + [vmem] * (len(operands) - prefetch),
        out_specs=vmem,
        scratch_shapes=list(scratch),
        compiler_params=pltpu.CompilerParams(vmem_limit_bytes=VMEM_LIMIT),
        cost_estimate=pl.CostEstimate(
            flops=flops, bytes_accessed=4 * 1024 * 1024, transcendentals=0
        ),
        name=name,
    )(*operands)


def shards(psi_first, psi_second, left_env, right_env, links):
    tiles, width, _ = psi_first.shape
    terms, lefts, _, _ = left_env.shape
    rights = right_env.shape[1]
    peers = lax.axis_size("sec")
    every = peers * tiles
    vector = lax.axis_index("v")
    swap = [(0, 1), (1, 0)]

    other_links = lax.ppermute(links, "v", swap)
    pieces = call(
        cut_kernel,
        (peers * 2 * tiles, width),
        prefetch=1,
        name="cut",
        operands=(
            vector.reshape(1).astype(jnp.int32),
            psi_first,
            psi_second,
            swap_order(2 * tiles, SLAB),
        ),
        flops=400_000_000,
    )
    pieces = lax.all_to_all(pieces, "sec", split_axis=0, concat_axis=0, tiled=True)
    other_left = lax.ppermute(left_env, "v", swap)
    other_right = lax.ppermute(right_env, "v", swap)
    wanted = jnp.stack([links.reshape(peers, tiles), other_links.reshape(peers, tiles)], axis=1)
    hot = (wanted.reshape(2 * every, 1) == jnp.arange(every)[None, :]).astype(jnp.bfloat16)
    chosen = call(
        choose_kernel,
        (2 * every, 2 * width),
        scratch=[pltpu.VMEM((every, 2 * width), jnp.bfloat16)],
        name="choose",
        operands=(pieces, hot, pick_parity(8 * tiles)),
        flops=700_000_000,
    )
    arrived = lax.all_to_all(chosen, "sec", split_axis=0, concat_axis=0, tiled=True)
    partial = call(
        apply_kernel,
        (tiles, width, width),
        scratch=[
            pltpu.VMEM((2, lefts, width, rights * width), jnp.bfloat16),
            pltpu.VMEM((rights, lefts * width, 2 * terms * width), jnp.bfloat16),
        ],
        name="apply",
        operands=(
            arrived,
            left_env,
            other_left,
            right_env,
            other_right,
            swap_order(SLAB, 2 * tiles),
        ),
        flops=2_000_000_000,
    )
    quarters = lax.axis_size("q")
    parts = lax.all_to_all(partial, "q", split_axis=0, concat_axis=0, tiled=True)
    parts = parts.reshape(quarters, tiles // quarters, width, width)
    mine = jnp.sum(parts.astype(jnp.float32), axis=0).astype(jnp.bfloat16)
    whole = lax.all_gather(mine, ("q", "v"), axis=0, tiled=False)
    whole = whole.reshape(quarters, 2, tiles // quarters, width, width)
    return (
        whole[:, 0].reshape(tiles, width, width),
        whole[:, 1].reshape(tiles, width, width),
    )


def solution(mesh):
    ops, secs = mesh.devices.shape
    grid = Mesh(mesh.devices.reshape(ops // 2, 2, secs), ("q", "v", "sec"))
    op = ("q", "v")
    in_specs = (
        P("sec", None, None),
        P("sec", None, None),
        P(op, "sec", None, None),
        P(op, None, None, None),
        P(op, None),
    )
    out_specs = (P("sec", None, None), P("sec", None, None))
    return jax.shard_map(shards, mesh=grid, in_specs=in_specs, out_specs=out_specs, check_vma=False)
```

```python
import jax
import jax.numpy as jnp
import numpy as np
from jax import lax
from jax.experimental import pallas as pl
from jax.experimental.pallas import tpu as pltpu
from jax.sharding import Mesh, PartitionSpec as P

VMEM_LIMIT = 30 * 1024 * 1024
VMEM_WHOLE = 60 * 1024 * 1024
SLAB = 16
CHUNKS = 4
SEC = ("chip", "core")


def dot(a, b):
    return jnp.dot(a, b, preferred_element_type=jnp.float32)


def swap_order(outer, inner):
    count = outer * inner
    matrix = np.zeros((count, count), np.float32)
    for o in range(outer):
        for i in range(inner):
            matrix[i * outer + o, o * inner + i] = 1
    return jnp.asarray(matrix, jnp.bfloat16)


def pick_parity(count):
    matrix = np.zeros((2, count, 2 * count), np.float32)
    for r in range(count):
        matrix[0, r, 2 * r] = 1
        matrix[1, r, 2 * r + 1] = 1
    return jnp.asarray(matrix, jnp.bfloat16)


def cut_kernel(first_ref, second_ref, order_ref, out_ref, held, order, sems):
    tiles, width, _ = first_ref.shape
    half = width // 2
    vector = lax.axis_index("v")
    order_copy = pltpu.make_async_copy(order_ref, order, sems.at[0])

    def fetch(source, chunk):
        count = tiles // CHUNKS
        span = pl.ds(chunk * count, count)
        return pltpu.make_async_copy(source.at[span], held.at[span], sems.at[1 + chunk])

    order_copy.start()
    for number, source in enumerate((first_ref, second_ref)):

        @pl.when(vector == number)
        def _():
            for chunk in range(CHUNKS):
                fetch(source, chunk).start()

    order_copy.wait()
    for chunk in range(CHUNKS):
        fetch(first_ref, chunk).wait()
    rows = 2 * tiles * SLAB
    for slab in range(half // SLAB):
        parts = []
        for k in range(tiles):
            for top in range(2):
                start = top * half + slab * SLAB
                parts.append(held[k, start : start + SLAB, :])
        block = dot(order[...], jnp.concatenate(parts, axis=0))
        out_ref[slab * rows : (slab + 1) * rows, :] = block.astype(jnp.bfloat16)


def choose_kernel(pieces_ref, hot_ref, parity_ref, out_ref, wide):
    count = parity_ref.shape[1]
    lanes = pieces_ref.shape[1]
    for b in range(pieces_ref.shape[0] // (2 * count)):
        block = pieces_ref[2 * count * b : 2 * count * (b + 1), :]
        for top in range(2):
            picked = dot(parity_ref[top], block).astype(jnp.bfloat16)
            wide[count * b : count * (b + 1), top * lanes : (top + 1) * lanes] = picked
    step = 256
    for m in range(hot_ref.shape[0] // step):
        out_ref[m * step : (m + 1) * step, :] = dot(
            hot_ref[m * step : (m + 1) * step, :], wide[...]
        ).astype(jnp.bfloat16)


def apply_kernel(
    arrived_ref,
    left_a,
    left_b,
    right_a,
    near_ref,
    far_ref,
    order_ref,
    out_ref,
    tiles,
    halves,
):
    terms, lefts, width, _ = left_a.shape
    rights = right_a.shape[1]
    upper = near_ref.shape[1]
    half = width // 2
    units = 2 * lefts * rights
    rows = units * SLAB
    second = lax.axis_index("core") == 1
    for slab in range(half // SLAB):
        block = dot(order_ref[...], arrived_ref[slab * rows : (slab + 1) * rows, :])
        block = block.astype(jnp.bfloat16)
        for u in range(units):
            g, a, r = u // (lefts * rights), u // rights % lefts, u % rights
            for top in range(2):
                tiles[
                    g,
                    a,
                    top * half + slab * SLAB : top * half + (slab + 1) * SLAB,
                    r * width : (r + 1) * width,
                ] = block[u * SLAB : (u + 1) * SLAB, top * width : (top + 1) * width]
    for g, left in enumerate((left_a, left_b)):
        for a in range(lefts):
            stacked = jnp.concatenate([left[t, a] for t in range(terms)], axis=0)
            product = dot(stacked, tiles[g, a]).astype(jnp.bfloat16)
            for t in range(terms):
                for r in range(rights):
                    column = (g * terms + t) * width
                    halves[r, a * width : (a + 1) * width, column : column + width] = product[
                        t * width : (t + 1) * width, r * width : (r + 1) * width
                    ]
    for r in range(rights):
        side = 0 if r < upper else 1
        place = r - side * (rights - upper)
        mine, other = (near_ref, far_ref) if side == 0 else (far_ref, near_ref)
        stacked = jnp.concatenate(
            [right_a[t, r] for t in range(terms)]
            + [jnp.where(second, other[t, place], mine[t, place]) for t in range(terms)],
            axis=0,
        )
        total = dot(halves[r], stacked).astype(jnp.bfloat16)
        for a in range(lefts):
            out_ref[a * rights + r] = total[a * width : (a + 1) * width]


def call(kernel, shape, operands, fetched, scratch=(), name=None, flops=0, limit=VMEM_LIMIT):
    vmem = pl.BlockSpec(memory_space=pltpu.VMEM)
    anywhere = pl.BlockSpec(memory_space=pltpu.HBM)
    return pl.pallas_call(
        kernel,
        out_shape=jax.ShapeDtypeStruct(shape, jnp.bfloat16),
        in_specs=[anywhere] * fetched + [vmem] * (len(operands) - fetched),
        out_specs=vmem,
        scratch_shapes=list(scratch),
        compiler_params=pltpu.CompilerParams(vmem_limit_bytes=limit),
        cost_estimate=pl.CostEstimate(
            flops=flops, bytes_accessed=4 * 1024 * 1024, transcendentals=0
        ),
        name=name,
    )(*operands)


def shards(psi_first, psi_second, left_env, right_env, links):
    tiles, width, _ = psi_first.shape
    terms, lefts, _, _ = left_env.shape
    rights = right_env.shape[1]
    peers = lax.axis_size(SEC)
    every = peers * tiles
    swap = [(0, 1), (1, 0)]

    slab_rows = 2 * tiles * SLAB
    order_shape = pltpu.VMEM((slab_rows, slab_rows), jnp.bfloat16)

    upper = (rights + 1) // 2
    core = lax.axis_index("core")
    near = lax.dynamic_slice_in_dim(right_env, core * (rights - upper), upper, 1)
    near = lax.ppermute(near, "v", swap)
    far = lax.ppermute(near, "core", swap)
    other_links = lax.ppermute(links, "v", swap)
    pieces = call(
        cut_kernel,
        (peers * 2 * tiles, width),
        (psi_first, psi_second, swap_order(2 * tiles, SLAB)),
        3,
        scratch=[
            pltpu.VMEM((tiles, width, width), jnp.bfloat16),
            order_shape,
            pltpu.SemaphoreType.DMA((1 + CHUNKS,)),
        ],
        name="cut",
        limit=VMEM_WHOLE,
        flops=400_000_000,
    )
    pieces = lax.all_to_all(pieces, SEC, split_axis=0, concat_axis=0, tiled=True)
    other_left = lax.ppermute(left_env, "v", swap)
    wanted = jnp.stack([links.reshape(peers, tiles), other_links.reshape(peers, tiles)], axis=1)
    hot = (wanted.reshape(2 * every, 1) == jnp.arange(every)[None, :]).astype(jnp.bfloat16)
    chosen = call(
        choose_kernel,
        (2 * every, 2 * width),
        (pieces, hot, pick_parity(8 * tiles)),
        0,
        scratch=[pltpu.VMEM((every, 2 * width), jnp.bfloat16)],
        name="choose",
        flops=700_000_000,
    )
    chosen, other_left = lax.optimization_barrier((chosen, other_left))
    arrived = lax.all_to_all(chosen, SEC, split_axis=0, concat_axis=0, tiled=True)
    partial = call(
        apply_kernel,
        (tiles, width, width),
        (arrived, left_env, other_left, right_env, near, far, swap_order(SLAB, 2 * tiles)),
        0,
        scratch=[
            pltpu.VMEM((2, lefts, width, rights * width), jnp.bfloat16),
            pltpu.VMEM((rights, lefts * width, 2 * terms * width), jnp.bfloat16),
        ],
        name="apply",
        flops=2_000_000_000,
    )
    quarters = lax.axis_size("q")
    parts = lax.all_to_all(partial, "q", split_axis=0, concat_axis=0, tiled=True)
    parts = parts.reshape(quarters, tiles // quarters, width, width)
    mine = jnp.sum(parts.astype(jnp.float32), axis=0).astype(jnp.bfloat16)
    whole = lax.all_gather(mine, ("q", "v"), axis=0, tiled=False)
    whole = whole.reshape(quarters, 2, tiles // quarters, width, width)
    return (
        whole[:, 0].reshape(tiles, width, width),
        whole[:, 1].reshape(tiles, width, width),
    )


def solution(mesh):
    ops, secs = mesh.devices.shape
    grid = Mesh(mesh.devices.reshape(ops // 2, 2, secs // 2, 2), ("q", "v", "chip", "core"))
    op, sec = ("q", "v"), SEC
    in_specs = (
        P(sec, None, None),
        P(sec, None, None),
        P(op, sec, None, None),
        P(op, None, None, None),
        P(op, None),
    )
    out_specs = (P(sec, None, None), P(sec, None, None))
    return jax.shard_map(shards, mesh=grid, in_specs=in_specs, out_specs=out_specs, check_vma=False)
```

```python
import jax
import jax.numpy as jnp
from jax import lax
from jax.experimental import pallas as pl
from jax.experimental.pallas import tpu as pltpu
from jax.sharding import Mesh, PartitionSpec as P

VMEM_LIMIT = 30 * 1024 * 1024
VMEM_WHOLE = 60 * 1024 * 1024
SLAB = 16
CHUNKS = 4
SEC = ("chip", "core")


def dot(a, b):
    return jnp.dot(a, b, preferred_element_type=jnp.float32)


def ones_where(condition):
    return jnp.where(condition, 1.0, 0.0).astype(jnp.bfloat16)


def iotas(rows, columns):
    shape = (rows, columns)
    return (
        lax.broadcasted_iota(jnp.int32, shape, 0),
        lax.broadcasted_iota(jnp.int32, shape, 1),
    )


def cut_kernel(first_ref, second_ref, out_ref, held, cut, fetch_sems, send_sems):
    tiles, width, _ = first_ref.shape
    half = width // 2
    slabs = half // SLAB
    rows = 2 * tiles * SLAB
    vector = lax.axis_index("v")

    def fetch(source, chunk):
        span = pl.ds(chunk * (tiles // CHUNKS), tiles // CHUNKS)
        return pltpu.make_async_copy(source.at[span], held.at[span], fetch_sems.at[chunk])

    def send(slab):
        return pltpu.make_async_copy(
            cut.at[slab], out_ref.at[pl.ds(slab * rows, rows)], send_sems.at[slab]
        )

    for number, source in enumerate((first_ref, second_ref)):

        @pl.when(vector == number)
        def _():
            for chunk in range(CHUNKS):
                fetch(source, chunk).start()

    unit = lax.broadcasted_iota(jnp.int32, (1, rows), 1)
    place, unit = unit % SLAB, unit // SLAB
    target = place * 2 * tiles + unit % tiles * 2 + unit // tiles
    order = ones_where(lax.broadcasted_iota(jnp.int32, (rows, rows), 0) == target)
    for chunk in range(CHUNKS):
        fetch(first_ref, chunk).wait()
    for slab in range(slabs):
        starts = [top * half + slab * SLAB for top in range(2)]
        block = jnp.concatenate(
            [held[k, start : start + SLAB, :] for start in starts for k in range(tiles)], axis=0
        )
        cut[slab] = dot(order, block).astype(jnp.bfloat16)
        send(slab).start()
    for slab in range(slabs):
        send(slab).wait()


def choose_kernel(pieces_ref, hot_ref, out_ref, wide):
    count = 96
    lanes = pieces_ref.shape[1]
    row, column = iotas(count, 2 * count)
    parity = [ones_where(column == 2 * row + top) for top in range(2)]
    for b in range(pieces_ref.shape[0] // (2 * count)):
        block = pieces_ref[2 * count * b : 2 * count * (b + 1), :]
        for top in range(2):
            picked = dot(parity[top], block).astype(jnp.bfloat16)
            wide[count * b : count * (b + 1), top * lanes : (top + 1) * lanes] = picked
    step = 256
    for m in range(hot_ref.shape[0] // step):
        out_ref[m * step : (m + 1) * step, :] = dot(
            hot_ref[m * step : (m + 1) * step, :], wide[...]
        ).astype(jnp.bfloat16)


def apply_kernel(
    arrived_ref,
    left_a,
    left_b,
    right_a,
    near_ref,
    far_ref,
    out_ref,
    tiles,
    halves,
):
    terms, lefts, width, _ = left_a.shape
    rights = right_a.shape[1]
    upper = near_ref.shape[1]
    half = width // 2
    units = 2 * lefts * rights
    part = SLAB // 2
    rows = units * part
    second = lax.axis_index("core") == 1
    row, column = iotas(rows, rows)
    order = ones_where(column == row % part * units + row // part)
    for slab in range(half // SLAB):
        blocks = [
            dot(order, arrived_ref[(2 * slab + p) * rows : (2 * slab + p + 1) * rows, :])
            for p in range(2)
        ]
        for u in range(units):
            g, a, r = u // (lefts * rights), u // rights % lefts, u % rights
            unit = jnp.concatenate([block[u * part : (u + 1) * part] for block in blocks], axis=0)
            unit = unit.astype(jnp.bfloat16)
            for top in range(2):
                tiles[
                    g,
                    a,
                    top * half + slab * SLAB : top * half + (slab + 1) * SLAB,
                    r * width : (r + 1) * width,
                ] = unit[:, top * width : (top + 1) * width]
    for g, left in enumerate((left_a, left_b)):
        for a in range(lefts):
            stacked = jnp.concatenate([left[t, a] for t in range(terms)], axis=0)
            product = dot(stacked, tiles[g, a]).astype(jnp.bfloat16)
            for t in range(terms):
                for r in range(rights):
                    column = (g * terms + t) * width
                    halves[r, a * width : (a + 1) * width, column : column + width] = product[
                        t * width : (t + 1) * width, r * width : (r + 1) * width
                    ]
    for r in range(rights):
        side = 0 if r < upper else 1
        place = r - side * (rights - upper)
        mine, other = (near_ref, far_ref) if side == 0 else (far_ref, near_ref)
        stacked = jnp.concatenate(
            [right_a[t, r] for t in range(terms)]
            + [jnp.where(second, other[t, place], mine[t, place]) for t in range(terms)],
            axis=0,
        )
        total = dot(halves[r], stacked).astype(jnp.bfloat16)
        for a in range(lefts):
            out_ref[a * rights + r] = total[a * width : (a + 1) * width]


def call(kernel, shape, operands, space, scratch=(), name=None, flops=0, limit=VMEM_LIMIT):
    spec = pl.BlockSpec(memory_space=space)
    return pl.pallas_call(
        kernel,
        out_shape=jax.ShapeDtypeStruct(shape, jnp.bfloat16),
        in_specs=[spec] * len(operands),
        out_specs=spec,
        scratch_shapes=list(scratch),
        compiler_params=pltpu.CompilerParams(vmem_limit_bytes=limit),
        cost_estimate=pl.CostEstimate(
            flops=flops, bytes_accessed=4 * 1024 * 1024, transcendentals=0
        ),
        name=name,
    )(*operands)


def shards(psi_first, psi_second, left_env, right_env, links):
    tiles, width, _ = psi_first.shape
    terms, lefts, _, _ = left_env.shape
    rights = right_env.shape[1]
    peers = lax.axis_size(SEC)
    every = peers * tiles
    swap = [(0, 1), (1, 0)]

    slabs = width // 2 // SLAB
    upper = (rights + 1) // 2
    core = lax.axis_index("core")

    other_links = lax.ppermute(links, "v", swap)
    pieces = call(
        cut_kernel,
        (peers * 2 * tiles, width),
        (psi_first, psi_second),
        pl.ANY,
        scratch=[
            pltpu.VMEM(psi_first.shape, jnp.bfloat16),
            pltpu.VMEM((slabs, 2 * tiles * SLAB, width), jnp.bfloat16),
            pltpu.SemaphoreType.DMA((CHUNKS,)),
            pltpu.SemaphoreType.DMA((slabs,)),
        ],
        name="cut",
        flops=400_000_000,
        limit=VMEM_WHOLE,
    )
    pieces = lax.all_to_all(pieces, SEC, split_axis=0, concat_axis=0, tiled=True)
    other_left = lax.ppermute(left_env, "v", swap)
    wanted = jnp.stack([links.reshape(peers, tiles), other_links.reshape(peers, tiles)], axis=1)
    hot = (wanted.reshape(2 * every, 1) == jnp.arange(every)[None, :]).astype(jnp.bfloat16)
    chosen = call(
        choose_kernel,
        (2 * every, 2 * width),
        (pieces, hot),
        pltpu.VMEM,
        scratch=[pltpu.VMEM((every, 2 * width), jnp.bfloat16)],
        name="choose",
        flops=700_000_000,
    )
    chosen, other_left = lax.optimization_barrier((chosen, other_left))
    arrived = lax.all_to_all(chosen, SEC, split_axis=0, concat_axis=0, tiled=True)
    near = lax.dynamic_slice_in_dim(right_env, core * (rights - upper), upper, 1)
    near = lax.ppermute(near, "v", swap)
    far = lax.ppermute(near, "core", swap)
    partial = call(
        apply_kernel,
        (tiles, width, width),
        (arrived, left_env, other_left, right_env, near, far),
        pltpu.VMEM,
        scratch=[
            pltpu.VMEM((2, lefts, width, rights * width), jnp.bfloat16),
            pltpu.VMEM((rights, lefts * width, 2 * terms * width), jnp.bfloat16),
        ],
        name="apply",
        flops=2_000_000_000,
    )
    quarters = lax.axis_size("q")
    parts = lax.all_to_all(partial, "q", split_axis=0, concat_axis=0, tiled=True)
    parts = parts.reshape(quarters, tiles // quarters, width, width)
    mine = jnp.sum(parts.astype(jnp.float32), axis=0).astype(jnp.bfloat16)
    own = lax.all_gather(mine, "q", axis=0, tiled=True)
    other = lax.ppermute(own, "v", swap)
    first = lax.axis_index("v") == 0
    return jnp.where(first, own, other), jnp.where(first, other, own)


def solution(mesh):
    ops, secs = mesh.devices.shape
    grid = Mesh(mesh.devices.reshape(ops // 2, 2, secs // 2, 2), ("q", "v", "chip", "core"))
    op, sec = ("q", "v"), SEC
    in_specs = (
        P(sec, None, None),
        P(sec, None, None),
        P(op, sec, None, None),
        P(op, None, None, None),
        P(op, None),
    )
    out_specs = (P(sec, None, None), P(sec, None, None))
    return jax.shard_map(shards, mesh=grid, in_specs=in_specs, out_specs=out_specs, check_vma=False)
```

```python
import functools

import jax
import jax.numpy as jnp
from jax import lax
from jax.experimental import pallas as pl
from jax.experimental.pallas import tpu as pltpu
from jax.sharding import Mesh, PartitionSpec as P

VMEM_LIMIT = 30 * 1024 * 1024
SLAB = 16
STEPS = 6
SEC = ("chip", "core")


def dot(a, b):
    return jnp.dot(a, b, preferred_element_type=jnp.float32)


def ones_where(condition):
    return jnp.where(condition, 1.0, 0.0).astype(jnp.bfloat16)


def iotas(rows, columns):
    shape = (rows, columns)
    return (
        lax.broadcasted_iota(jnp.int32, shape, 0),
        lax.broadcasted_iota(jnp.int32, shape, 1),
    )


def choose_kernel(pieces_ref, hot_ref, out_ref, wide, block, sems):
    count = 96
    lanes = pieces_ref.shape[1]
    row, column = iotas(count, 2 * count)
    parity = [ones_where(column == 2 * row + top) for top in range(2)]
    for b in range(pieces_ref.shape[0] // (2 * count)):
        pair = pieces_ref[2 * count * b : 2 * count * (b + 1), :]
        for top in range(2):
            picked = dot(parity[top], pair).astype(jnp.bfloat16)
            wide[count * b : count * (b + 1), top * lanes : (top + 1) * lanes] = picked
    steps, step, _ = block.shape

    def send(m):
        return pltpu.make_async_copy(block.at[m], out_ref.at[pl.ds(m * step, step)], sems.at[m])

    for m in range(steps):
        hot = hot_ref[m * step : (m + 1) * step, :]
        block[m] = dot(hot, wide[...]).astype(jnp.bfloat16)
        send(m).start()
    for m in range(steps):
        send(m).wait()


def apply_kernel(
    arrived_ref,
    left_a,
    left_b,
    right_a,
    near_ref,
    far_ref,
    out_ref,
    tiles,
    halves,
):
    terms, lefts, width, _ = left_a.shape
    rights = right_a.shape[1]
    upper = near_ref.shape[1]
    half = width // 2
    units = 2 * lefts * rights
    part = SLAB // 2
    rows = units * part
    second = lax.axis_index("core") == 1
    row, column = iotas(rows, rows)
    order = ones_where(column == row % part * units + row // part)
    for slab in range(half // SLAB):
        blocks = [
            dot(order, arrived_ref[(2 * slab + p) * rows : (2 * slab + p + 1) * rows, :])
            for p in range(2)
        ]
        for u in range(units):
            g, a, r = u // (lefts * rights), u // rights % lefts, u % rights
            unit = jnp.concatenate([block[u * part : (u + 1) * part] for block in blocks], axis=0)
            unit = unit.astype(jnp.bfloat16)
            for top in range(2):
                tiles[
                    g,
                    a,
                    top * half + slab * SLAB : top * half + (slab + 1) * SLAB,
                    r * width : (r + 1) * width,
                ] = unit[:, top * width : (top + 1) * width]
    for g, left in enumerate((left_a, left_b)):
        for a in range(lefts):
            stacked = jnp.concatenate([left[t, a] for t in range(terms)], axis=0)
            for pair in range(rights // 2):
                span = slice(2 * pair * width, 2 * (pair + 1) * width)
                product = dot(stacked, tiles[g, a, :, span]).astype(jnp.bfloat16)
                for t in range(terms):
                    for side in range(2):
                        column = (g * terms + t) * width
                        halves[
                            2 * pair + side, a * width : (a + 1) * width, column : column + width
                        ] = product[
                            t * width : (t + 1) * width, side * width : (side + 1) * width
                        ]
    for r in range(rights):
        side = 0 if r < upper else 1
        place = r - side * (rights - upper)
        mine, other = (near_ref, far_ref) if side == 0 else (far_ref, near_ref)
        stacked = jnp.concatenate(
            [right_a[t, r] for t in range(terms)]
            + [jnp.where(second, other[t, place], mine[t, place]) for t in range(terms)],
            axis=0,
        )
        total = dot(halves[r], stacked).astype(jnp.bfloat16)
        for a in range(lefts):
            out_ref[a * rights + r] = total[a * width : (a + 1) * width]


def place_kernel(number, data_ref, *refs):
    first_ref, second_ref, sems = refs[-3:]
    turn = (lax.axis_index("v") + number) % 2
    chunks = sems.shape[0]
    count = data_ref.shape[0] // chunks

    def move(target, chunk):
        span = pl.ds(chunk * count, count)
        return pltpu.make_async_copy(data_ref.at[span], target.at[span], sems.at[chunk])

    for side, target in enumerate((first_ref, second_ref)):

        @pl.when(turn == side)
        def _():
            for chunk in range(chunks):
                move(target, chunk).start()

    for chunk in range(chunks):
        move(first_ref, chunk).wait()


def place(number, data, *ends):
    end = jax.ShapeDtypeStruct(data.shape, jnp.bfloat16)
    return pl.pallas_call(
        functools.partial(place_kernel, number),
        out_shape=(end, end),
        in_specs=[pl.BlockSpec(memory_space=pltpu.VMEM)]
        + [pl.BlockSpec(memory_space=pl.ANY)] * len(ends),
        out_specs=(pl.BlockSpec(memory_space=pl.ANY),) * 2,
        scratch_shapes=[pltpu.SemaphoreType.DMA((4,))],
        input_output_aliases={1: 0, 2: 1} if ends else {},
        compiler_params=pltpu.CompilerParams(vmem_limit_bytes=VMEM_LIMIT),
        name="place",
    )(data, *ends)


def call(kernel, shape, operands, space, scratch=(), name=None, flops=0, limit=VMEM_LIMIT, out_space=None):
    spec = pl.BlockSpec(memory_space=space)
    out_spec = pl.BlockSpec(memory_space=out_space or space)
    return pl.pallas_call(
        kernel,
        out_shape=jax.ShapeDtypeStruct(shape, jnp.bfloat16),
        in_specs=[spec] * len(operands),
        out_specs=out_spec,
        scratch_shapes=list(scratch),
        compiler_params=pltpu.CompilerParams(vmem_limit_bytes=limit),
        cost_estimate=pl.CostEstimate(
            flops=flops, bytes_accessed=4 * 1024 * 1024, transcendentals=0
        ),
        name=name,
    )(*operands)


def shards(psi_first, psi_second, left_env, right_env, links):
    tiles, width, _ = psi_first.shape
    terms, lefts, _, _ = left_env.shape
    rights = right_env.shape[1]
    peers = lax.axis_size(SEC)
    every = peers * tiles
    swap = [(0, 1), (1, 0)]

    upper = (rights + 1) // 2
    core = lax.axis_index("core")

    other_links = lax.ppermute(links, "v", swap)
    chosen_psi = jnp.where(lax.axis_index("v") == 0, psi_first, psi_second)
    pieces = chosen_psi.reshape(tiles, 2, width // 2, width).transpose(2, 0, 1, 3)
    pieces = pieces.reshape(peers * 2 * tiles, width)
    pieces = lax.all_to_all(pieces, SEC, split_axis=0, concat_axis=0, tiled=True)
    other_left = lax.ppermute(left_env, "v", swap)
    wanted = jnp.stack([links.reshape(peers, tiles), other_links.reshape(peers, tiles)], axis=1)
    hot = (wanted.reshape(2 * every, 1) == jnp.arange(every)[None, :]).astype(jnp.bfloat16)
    chosen = call(
        choose_kernel,
        (2 * every, 2 * width),
        (pieces, hot),
        pltpu.VMEM,
        scratch=[
            pltpu.VMEM((every, 2 * width), jnp.bfloat16),
            pltpu.VMEM((STEPS, 2 * every // STEPS, 2 * width), jnp.bfloat16),
            pltpu.SemaphoreType.DMA((STEPS,)),
        ],
        name="choose",
        out_space=pl.ANY,
        flops=700_000_000,
    )
    chosen, other_left = lax.optimization_barrier((chosen, other_left))
    arrived = lax.all_to_all(chosen, SEC, split_axis=0, concat_axis=0, tiled=True)
    near = lax.dynamic_slice_in_dim(right_env, core * (rights - upper), upper, 1)
    near = lax.ppermute(near, "v", swap)
    far = lax.ppermute(near, "core", swap)
    partial = call(
        apply_kernel,
        (tiles, width, width),
        (arrived, left_env, other_left, right_env, near, far),
        pltpu.VMEM,
        scratch=[
            pltpu.VMEM((2, lefts, width, rights * width), jnp.bfloat16),
            pltpu.VMEM((rights, lefts * width, 2 * terms * width), jnp.bfloat16),
        ],
        name="apply",
        flops=2_000_000_000,
    )
    quarters = lax.axis_size("q")
    parts = lax.all_to_all(partial, "q", split_axis=0, concat_axis=0, tiled=True)
    parts = parts.reshape(quarters, tiles // quarters, width, width)
    mine = jnp.sum(parts.astype(jnp.float32), axis=0).astype(jnp.bfloat16)
    own = lax.all_gather(mine, "q", axis=0, tiled=True)
    other = lax.ppermute(own, "v", swap)
    return place(1, other, *place(0, own))


def solution(mesh):
    ops, secs = mesh.devices.shape
    grid = Mesh(mesh.devices.reshape(ops // 2, 2, secs // 2, 2), ("q", "v", "chip", "core"))
    op, sec = ("q", "v"), SEC
    in_specs = (
        P(sec, None, None),
        P(sec, None, None),
        P(op, sec, None, None),
        P(op, None, None, None),
        P(op, None),
    )
    out_specs = (P(sec, None, None), P(sec, None, None))
    return jax.shard_map(shards, mesh=grid, in_specs=in_specs, out_specs=out_specs, check_vma=False)
```

```python
import functools

import jax
import jax.numpy as jnp
from jax import lax
from jax.experimental import pallas as pl
from jax.experimental.pallas import tpu as pltpu
from jax.sharding import Mesh, PartitionSpec as P

VMEM_LIMIT = 30 * 1024 * 1024
SLAB = 16
STEPS = 6
SEC = ("chip", "core")


def dot(a, b):
    return jnp.dot(a, b, preferred_element_type=jnp.float32)


def ones_where(condition):
    return jnp.where(condition, 1.0, 0.0).astype(jnp.bfloat16)


def iotas(rows, columns):
    shape = (rows, columns)
    return (
        lax.broadcasted_iota(jnp.int32, shape, 0),
        lax.broadcasted_iota(jnp.int32, shape, 1),
    )


def choose_kernel(pieces_ref, hot_ref, out_ref, wide, block, sems):
    count = 96
    lanes = pieces_ref.shape[1]
    row, column = iotas(count, 2 * count)
    parity = [ones_where(column == 2 * row + top) for top in range(2)]
    for b in range(pieces_ref.shape[0] // (2 * count)):
        pair = pieces_ref[2 * count * b : 2 * count * (b + 1), :]
        for top in range(2):
            picked = dot(parity[top], pair).astype(jnp.bfloat16)
            wide[count * b : count * (b + 1), top * lanes : (top + 1) * lanes] = picked
    steps, step, _ = block.shape

    def send(m):
        return pltpu.make_async_copy(block.at[m], out_ref.at[pl.ds(m * step, step)], sems.at[m])

    for m in range(steps):
        hot = hot_ref[m * step : (m + 1) * step, :]
        block[m] = dot(hot, wide[...]).astype(jnp.bfloat16)
        send(m).start()
    for m in range(steps):
        send(m).wait()


def apply_kernel(
    arrived_ref,
    left_a,
    left_b,
    right_a,
    near_ref,
    far_ref,
    out_ref,
    tiles,
    halves,
):
    terms, lefts, width, _ = left_a.shape
    rights = right_a.shape[1]
    upper = near_ref.shape[1]
    half = width // 2
    units = 2 * lefts * rights
    part = SLAB // 2
    rows = units * part
    second = lax.axis_index("core") == 1
    row, column = iotas(rows, rows)
    order = ones_where(column == row % part * units + row // part)
    for slab in range(half // SLAB):
        blocks = [
            dot(order, arrived_ref[(2 * slab + p) * rows : (2 * slab + p + 1) * rows, :])
            for p in range(2)
        ]
        for u in range(units):
            g, a, r = u // (lefts * rights), u // rights % lefts, u % rights
            unit = jnp.concatenate([block[u * part : (u + 1) * part] for block in blocks], axis=0)
            unit = unit.astype(jnp.bfloat16)
            for top in range(2):
                tiles[
                    g,
                    a,
                    top * half + slab * SLAB : top * half + (slab + 1) * SLAB,
                    r * width : (r + 1) * width,
                ] = unit[:, top * width : (top + 1) * width]
    for g, left in enumerate((left_a, left_b)):
        for a in range(lefts):
            stacked = jnp.concatenate([left[t, a] for t in range(terms)], axis=0)
            for pair in range(rights // 2):
                span = slice(2 * pair * width, 2 * (pair + 1) * width)
                product = dot(stacked, tiles[g, a, :, span]).astype(jnp.bfloat16)
                for t in range(terms):
                    for side in range(2):
                        column = (g * terms + t) * width
                        halves[
                            2 * pair + side, a * width : (a + 1) * width, column : column + width
                        ] = product[
                            t * width : (t + 1) * width, side * width : (side + 1) * width
                        ]
    for r in range(rights):
        side = 0 if r < upper else 1
        place = r - side * (rights - upper)
        mine, other = (near_ref, far_ref) if side == 0 else (far_ref, near_ref)
        stacked = jnp.concatenate(
            [right_a[t, r] for t in range(terms)]
            + [jnp.where(second, other[t, place], mine[t, place]) for t in range(terms)],
            axis=0,
        )
        total = dot(halves[r], stacked).astype(jnp.bfloat16)
        for a in range(lefts):
            out_ref[a * rights + r] = total[a * width : (a + 1) * width]


def place_kernel(number, data_ref, *refs):
    first_ref, second_ref, sems = refs[-3:]
    turn = (lax.axis_index("v") + number) % 2
    chunks = sems.shape[0]
    count = data_ref.shape[0] // chunks

    def move(target, chunk):
        span = pl.ds(chunk * count, count)
        return pltpu.make_async_copy(data_ref.at[span], target.at[span], sems.at[chunk])

    for side, target in enumerate((first_ref, second_ref)):

        @pl.when(turn == side)
        def _():
            for chunk in range(chunks):
                move(target, chunk).start()

    for chunk in range(chunks):
        move(first_ref, chunk).wait()


def place(number, data, *ends):
    end = jax.ShapeDtypeStruct(data.shape, jnp.bfloat16)
    return pl.pallas_call(
        functools.partial(place_kernel, number),
        out_shape=(end, end),
        in_specs=[pl.BlockSpec(memory_space=pltpu.VMEM)]
        + [pl.BlockSpec(memory_space=pl.ANY)] * len(ends),
        out_specs=(pl.BlockSpec(memory_space=pl.ANY),) * 2,
        scratch_shapes=[pltpu.SemaphoreType.DMA((4,))],
        input_output_aliases={1: 0, 2: 1} if ends else {},
        compiler_params=pltpu.CompilerParams(vmem_limit_bytes=VMEM_LIMIT),
        name="place",
    )(data, *ends)


def call(kernel, shape, operands, space, scratch=(), name=None, flops=0, limit=VMEM_LIMIT, out_space=None):
    spec = pl.BlockSpec(memory_space=space)
    out_spec = pl.BlockSpec(memory_space=out_space or space)
    return pl.pallas_call(
        kernel,
        out_shape=jax.ShapeDtypeStruct(shape, jnp.bfloat16),
        in_specs=[spec] * len(operands),
        out_specs=out_spec,
        scratch_shapes=list(scratch),
        compiler_params=pltpu.CompilerParams(vmem_limit_bytes=limit),
        cost_estimate=pl.CostEstimate(
            flops=flops, bytes_accessed=4 * 1024 * 1024, transcendentals=0
        ),
        name=name,
    )(*operands)


def shards(psi_first, psi_second, left_env, right_env, links):
    tiles, width, _ = psi_first.shape
    terms, lefts, _, _ = left_env.shape
    rights = right_env.shape[1]
    peers = lax.axis_size(SEC)
    every = peers * tiles
    swap = [(0, 1), (1, 0)]

    upper = (rights + 1) // 2
    core = lax.axis_index("core")

    other_links = lax.ppermute(links, "v", swap)
    chosen_psi = jnp.where(lax.axis_index("v") == 0, psi_first, psi_second)
    pieces = chosen_psi.reshape(tiles, 2, width // 2, width).transpose(2, 0, 1, 3)
    pieces = pieces.reshape(peers * 2 * tiles, width)
    pieces = lax.all_to_all(pieces, SEC, split_axis=0, concat_axis=0, tiled=True)
    other_left = lax.ppermute(left_env, "v", swap)
    wanted = jnp.stack([links.reshape(peers, tiles), other_links.reshape(peers, tiles)], axis=1)
    hot = (wanted.reshape(2 * every, 1) == jnp.arange(every)[None, :]).astype(jnp.bfloat16)
    chosen = call(
        choose_kernel,
        (2 * every, 2 * width),
        (pieces, hot),
        pltpu.VMEM,
        scratch=[
            pltpu.VMEM((every, 2 * width), jnp.bfloat16),
            pltpu.VMEM((STEPS, 2 * every // STEPS, 2 * width), jnp.bfloat16),
            pltpu.SemaphoreType.DMA((STEPS,)),
        ],
        name="choose",
        out_space=pl.ANY,
        flops=700_000_000,
    )
    chosen, other_left = lax.optimization_barrier((chosen, other_left))
    arrived = lax.all_to_all(chosen, SEC, split_axis=0, concat_axis=0, tiled=True)
    near = lax.dynamic_slice_in_dim(right_env, core * (rights - upper), upper, 1)
    near = lax.ppermute(near, "v", swap)
    far = lax.ppermute(near, "core", swap)
    partial = call(
        apply_kernel,
        (tiles, width, width),
        (arrived, left_env, other_left, right_env, near, far),
        pltpu.VMEM,
        scratch=[
            pltpu.VMEM((2, lefts, width, rights * width), jnp.bfloat16),
            pltpu.VMEM((rights, lefts * width, 2 * terms * width), jnp.bfloat16),
        ],
        name="apply",
        flops=2_000_000_000,
    )
    quarters = lax.axis_size("q")
    axes = ("q", "v", "core")
    sets = [
        [(q * 2 + v) * 2 + c for q in (range(quarters) if c == 0 else reversed(range(quarters)))]
        for v in range(2)
        for c in range(2)
    ]
    parts = lax.all_to_all(
        partial, axes, split_axis=0, concat_axis=0, tiled=True, axis_index_groups=sets
    )
    parts = parts.reshape(quarters, tiles // quarters, width, width)
    mine = jnp.sum(parts.astype(jnp.float32), axis=0).astype(jnp.bfloat16)
    own = lax.all_gather(mine, axes, axis=0, tiled=True, axis_index_groups=sets)
    other = lax.ppermute(own, "v", swap)
    return place(1, other, *place(0, own))


def solution(mesh):
    ops, secs = mesh.devices.shape
    grid = Mesh(mesh.devices.reshape(ops // 2, 2, secs // 2, 2), ("q", "v", "chip", "core"))
    op, sec = ("q", "v"), SEC
    in_specs = (
        P(sec, None, None),
        P(sec, None, None),
        P(op, sec, None, None),
        P(op, None, None, None),
        P(op, None),
    )
    out_specs = (P(sec, None, None), P(sec, None, None))
    return jax.shard_map(shards, mesh=grid, in_specs=in_specs, out_specs=out_specs, check_vma=False)
```

```python
import functools

import jax
import jax.numpy as jnp
from jax import lax
from jax.experimental import pallas as pl
from jax.experimental.pallas import tpu as pltpu
from jax.sharding import Mesh, PartitionSpec as P

VMEM_LIMIT = 30 * 1024 * 1024
SLAB = 16
STEPS = 6
SEC = ("chip", "core")


def dot(a, b):
    return jnp.dot(a, b, preferred_element_type=jnp.float32)


def ones_where(condition):
    return jnp.where(condition, 1.0, 0.0).astype(jnp.bfloat16)


def iotas(rows, columns):
    shape = (rows, columns)
    return (
        lax.broadcasted_iota(jnp.int32, shape, 0),
        lax.broadcasted_iota(jnp.int32, shape, 1),
    )


def choose_kernel(pieces_ref, hot_ref, out_ref, wide, block, sems):
    count = 96
    lanes = pieces_ref.shape[1]
    row, column = iotas(count, 2 * count)
    parity = [ones_where(column == 2 * row + top) for top in range(2)]
    for b in range(pieces_ref.shape[0] // (2 * count)):
        pair = pieces_ref[2 * count * b : 2 * count * (b + 1), :]
        for top in range(2):
            picked = dot(parity[top], pair).astype(jnp.bfloat16)
            wide[count * b : count * (b + 1), top * lanes : (top + 1) * lanes] = picked
    steps, step, _ = block.shape

    def send(m):
        return pltpu.make_async_copy(block.at[m], out_ref.at[pl.ds(m * step, step)], sems.at[m])

    for m in range(steps):
        hot = hot_ref[m * step : (m + 1) * step, :]
        block[m] = dot(hot, wide[...]).astype(jnp.bfloat16)
        send(m).start()
    for m in range(steps):
        send(m).wait()


def apply_kernel(
    arrived_ref,
    left_a,
    left_b,
    right_a,
    near_ref,
    far_ref,
    out_ref,
    tiles,
    halves,
):
    terms, lefts, width, _ = left_a.shape
    rights = right_a.shape[1]
    upper = near_ref.shape[1]
    half = width // 2
    units = 2 * lefts * rights
    part = SLAB // 2
    rows = units * part
    second = lax.axis_index("core") == 1
    row, column = iotas(rows, rows)
    order = ones_where(column == row % part * units + row // part)
    for slab in range(half // SLAB):
        blocks = [
            dot(order, arrived_ref[(2 * slab + p) * rows : (2 * slab + p + 1) * rows, :])
            for p in range(2)
        ]
        for u in range(units):
            g, a, r = u // (lefts * rights), u // rights % lefts, u % rights
            unit = jnp.concatenate([block[u * part : (u + 1) * part] for block in blocks], axis=0)
            unit = unit.astype(jnp.bfloat16)
            for top in range(2):
                tiles[
                    g,
                    a,
                    top * half + slab * SLAB : top * half + (slab + 1) * SLAB,
                    r * width : (r + 1) * width,
                ] = unit[:, top * width : (top + 1) * width]
    for g, left in enumerate((left_a, left_b)):
        for a in range(lefts):
            stacked = jnp.concatenate([left[t, a] for t in range(terms)], axis=0)
            for pair in range(rights // 2):
                span = slice(2 * pair * width, 2 * (pair + 1) * width)
                product = dot(stacked, tiles[g, a, :, span]).astype(jnp.bfloat16)
                for t in range(terms):
                    for side in range(2):
                        column = (g * terms + t) * width
                        halves[
                            2 * pair + side, a * width : (a + 1) * width, column : column + width
                        ] = product[
                            t * width : (t + 1) * width, side * width : (side + 1) * width
                        ]
    for r in range(rights):
        side = 0 if r < upper else 1
        place = r - side * (rights - upper)
        mine, other = (near_ref, far_ref) if side == 0 else (far_ref, near_ref)
        stacked = jnp.concatenate(
            [right_a[t, r] for t in range(terms)]
            + [jnp.where(second, other[t, place], mine[t, place]) for t in range(terms)],
            axis=0,
        )
        total = dot(halves[r], stacked).astype(jnp.bfloat16)
        for a in range(lefts):
            out_ref[a * rights + r] = total[a * width : (a + 1) * width]


def place_kernel(number, data_ref, *refs):
    first_ref, second_ref, sems = refs[-3:]
    turn = (lax.axis_index("v") + number) % 2
    chunks = sems.shape[0]
    count = data_ref.shape[0] // chunks

    def move(target, chunk):
        span = pl.ds(chunk * count, count)
        return pltpu.make_async_copy(data_ref.at[span], target.at[span], sems.at[chunk])

    for side, target in enumerate((first_ref, second_ref)):

        @pl.when(turn == side)
        def _():
            for chunk in range(chunks):
                move(target, chunk).start()

    for chunk in range(chunks):
        move(first_ref, chunk).wait()


def place(number, data, *ends):
    end = jax.ShapeDtypeStruct(data.shape, jnp.bfloat16)
    return pl.pallas_call(
        functools.partial(place_kernel, number),
        out_shape=(end, end),
        in_specs=[pl.BlockSpec(memory_space=pltpu.VMEM)]
        + [pl.BlockSpec(memory_space=pl.ANY)] * len(ends),
        out_specs=(pl.BlockSpec(memory_space=pl.ANY),) * 2,
        scratch_shapes=[pltpu.SemaphoreType.DMA((4,))],
        input_output_aliases={1: 0, 2: 1} if ends else {},
        compiler_params=pltpu.CompilerParams(vmem_limit_bytes=VMEM_LIMIT),
        name="place",
    )(data, *ends)


def call(kernel, shape, operands, space, scratch=(), name=None, flops=0, limit=VMEM_LIMIT, out_space=None):
    spec = pl.BlockSpec(memory_space=space)
    out_spec = pl.BlockSpec(memory_space=out_space or space)
    return pl.pallas_call(
        kernel,
        out_shape=jax.ShapeDtypeStruct(shape, jnp.bfloat16),
        in_specs=[spec] * len(operands),
        out_specs=out_spec,
        scratch_shapes=list(scratch),
        compiler_params=pltpu.CompilerParams(vmem_limit_bytes=limit),
        cost_estimate=pl.CostEstimate(
            flops=flops, bytes_accessed=4 * 1024 * 1024, transcendentals=0
        ),
        name=name,
    )(*operands)


def shards(psi_first, psi_second, left_env, right_env, links):
    tiles, width, _ = psi_first.shape
    terms, lefts, _, _ = left_env.shape
    rights = right_env.shape[1]
    peers = lax.axis_size(SEC)
    every = peers * tiles
    swap = [(0, 1), (1, 0)]

    upper = (rights + 1) // 2
    core = lax.axis_index("core")

    other_links = lax.ppermute(links, "v", swap)
    chosen_psi = jnp.where(lax.axis_index("v") == 0, psi_first, psi_second)
    pieces = chosen_psi.reshape(tiles, 2, width // 2, width).transpose(2, 0, 1, 3)
    pieces = pieces.reshape(peers * 2 * tiles, width)
    pieces = lax.all_to_all(pieces, SEC, split_axis=0, concat_axis=0, tiled=True)
    other_left = lax.ppermute(left_env, "v", swap)
    wanted = jnp.stack([links.reshape(peers, tiles), other_links.reshape(peers, tiles)], axis=1)
    hot = (wanted.reshape(2 * every, 1) == jnp.arange(every)[None, :]).astype(jnp.bfloat16)
    chosen = call(
        choose_kernel,
        (2 * every, 2 * width),
        (pieces, hot),
        pltpu.VMEM,
        scratch=[
            pltpu.VMEM((every, 2 * width), jnp.bfloat16),
            pltpu.VMEM((STEPS, 2 * every // STEPS, 2 * width), jnp.bfloat16),
            pltpu.SemaphoreType.DMA((STEPS,)),
        ],
        name="choose",
        out_space=pl.ANY,
        flops=700_000_000,
    )
    chosen, other_left = lax.optimization_barrier((chosen, other_left))
    arrived = lax.all_to_all(chosen, SEC, split_axis=0, concat_axis=0, tiled=True)
    near = lax.dynamic_slice_in_dim(right_env, core * (rights - upper), upper, 1)
    near = lax.ppermute(near, "v", swap)
    far = lax.ppermute(near, "core", swap)
    partial = call(
        apply_kernel,
        (tiles, width, width),
        (arrived, left_env, other_left, right_env, near, far),
        pltpu.VMEM,
        scratch=[
            pltpu.VMEM((2, lefts, width, rights * width), jnp.bfloat16),
            pltpu.VMEM((rights, lefts * width, 2 * terms * width), jnp.bfloat16),
        ],
        name="apply",
        flops=2_000_000_000,
    )
    quarters = lax.axis_size("q")
    axes = ("q", "v", "core")
    sets = [
        [(q * 2 + v) * 2 + c for q in (range(quarters) if c == 1 else reversed(range(quarters)))]
        for v in range(2)
        for c in range(2)
    ]
    parts = lax.all_to_all(
        partial, axes, split_axis=0, concat_axis=0, tiled=True, axis_index_groups=sets
    )
    parts = parts.reshape(quarters, tiles // quarters, width, width)
    mine = jnp.sum(parts.astype(jnp.float32), axis=0).astype(jnp.bfloat16)
    own = lax.all_gather(mine, axes, axis=0, tiled=True, axis_index_groups=sets)
    other = lax.ppermute(own, "v", swap)
    return place(1, other, *place(0, own))


def solution(mesh):
    ops, secs = mesh.devices.shape
    grid = Mesh(mesh.devices.reshape(ops // 2, 2, secs // 2, 2), ("q", "v", "chip", "core"))
    op, sec = ("q", "v"), SEC
    in_specs = (
        P(sec, None, None),
        P(sec, None, None),
        P(op, sec, None, None),
        P(op, None, None, None),
        P(op, None),
    )
    out_specs = (P(sec, None, None), P(sec, None, None))
    return jax.shard_map(shards, mesh=grid, in_specs=in_specs, out_specs=out_specs, check_vma=False)
```

```python
import functools

import jax
import jax.numpy as jnp
from jax import lax
from jax.experimental import pallas as pl
from jax.experimental.pallas import tpu as pltpu
from jax.sharding import Mesh, PartitionSpec as P

VMEM_LIMIT = 30 * 1024 * 1024
SLAB = 16
STEPS = 12
SEC = ("chip", "core")


def dot(a, b):
    return jnp.dot(a, b, preferred_element_type=jnp.float32)


def ones_where(condition):
    return jnp.where(condition, 1.0, 0.0).astype(jnp.bfloat16)


def iotas(rows, columns):
    shape = (rows, columns)
    return (
        lax.broadcasted_iota(jnp.int32, shape, 0),
        lax.broadcasted_iota(jnp.int32, shape, 1),
    )


def choose_kernel(pieces_ref, hot_ref, out_ref, wide, block, sems):
    count = 96
    lanes = pieces_ref.shape[1]
    row, column = iotas(count, 2 * count)
    parity = [ones_where(column == 2 * row + top) for top in range(2)]
    for b in range(pieces_ref.shape[0] // (2 * count)):
        pair = pieces_ref[2 * count * b : 2 * count * (b + 1), :]
        for top in range(2):
            picked = dot(parity[top], pair).astype(jnp.bfloat16)
            wide[count * b : count * (b + 1), top * lanes : (top + 1) * lanes] = picked
    steps, step, _ = block.shape

    def send(m):
        return pltpu.make_async_copy(block.at[m], out_ref.at[pl.ds(m * step, step)], sems.at[m])

    for m in range(steps):
        hot = hot_ref[m * step : (m + 1) * step, :]
        block[m] = dot(hot, wide[...]).astype(jnp.bfloat16)
        send(m).start()
    for m in range(steps):
        send(m).wait()


def apply_kernel(
    arrived_ref,
    left_a,
    left_b,
    right_a,
    near_ref,
    far_ref,
    out_ref,
    tiles,
    halves,
):
    terms, lefts, width, _ = left_a.shape
    rights = right_a.shape[1]
    upper = near_ref.shape[1]
    half = width // 2
    units = 2 * lefts * rights
    part = SLAB // 2
    rows = units * part
    second = lax.axis_index("core") == 1
    row, column = iotas(rows, rows)
    order = ones_where(column == row % part * units + row // part)
    for slab in range(half // SLAB):
        blocks = [
            dot(order, arrived_ref[(2 * slab + p) * rows : (2 * slab + p + 1) * rows, :])
            for p in range(2)
        ]
        for u in range(units):
            g, a, r = u // (lefts * rights), u // rights % lefts, u % rights
            unit = jnp.concatenate([block[u * part : (u + 1) * part] for block in blocks], axis=0)
            unit = unit.astype(jnp.bfloat16)
            for top in range(2):
                tiles[
                    g,
                    a,
                    top * half + slab * SLAB : top * half + (slab + 1) * SLAB,
                    r * width : (r + 1) * width,
                ] = unit[:, top * width : (top + 1) * width]
    for g, left in enumerate((left_a, left_b)):
        for a in range(lefts):
            stacked = jnp.concatenate([left[t, a] for t in range(terms)], axis=0)
            for pair in range(rights // 2):
                span = slice(2 * pair * width, 2 * (pair + 1) * width)
                product = dot(stacked, tiles[g, a, :, span]).astype(jnp.bfloat16)
                for t in range(terms):
                    for side in range(2):
                        column = (g * terms + t) * width
                        halves[
                            2 * pair + side, a * width : (a + 1) * width, column : column + width
                        ] = product[
                            t * width : (t + 1) * width, side * width : (side + 1) * width
                        ]
    for r in range(rights):
        side = 0 if r < upper else 1
        place = r - side * (rights - upper)
        mine, other = (near_ref, far_ref) if side == 0 else (far_ref, near_ref)
        stacked = jnp.concatenate(
            [right_a[t, r] for t in range(terms)]
            + [jnp.where(second, other[t, place], mine[t, place]) for t in range(terms)],
            axis=0,
        )
        total = dot(halves[r], stacked).astype(jnp.bfloat16)
        for a in range(lefts):
            out_ref[a * rights + r] = total[a * width : (a + 1) * width]


def place_kernel(number, data_ref, *refs):
    first_ref, second_ref, sems = refs[-3:]
    turn = (lax.axis_index("v") + number) % 2
    chunks = sems.shape[0]
    count = data_ref.shape[0] // chunks

    def move(target, chunk):
        span = pl.ds(chunk * count, count)
        return pltpu.make_async_copy(data_ref.at[span], target.at[span], sems.at[chunk])

    for side, target in enumerate((first_ref, second_ref)):

        @pl.when(turn == side)
        def _():
            for chunk in range(chunks):
                move(target, chunk).start()

    for chunk in range(chunks):
        move(first_ref, chunk).wait()


def place(number, data, *ends):
    end = jax.ShapeDtypeStruct(data.shape, jnp.bfloat16)
    return pl.pallas_call(
        functools.partial(place_kernel, number),
        out_shape=(end, end),
        in_specs=[pl.BlockSpec(memory_space=pltpu.VMEM)]
        + [pl.BlockSpec(memory_space=pl.ANY)] * len(ends),
        out_specs=(pl.BlockSpec(memory_space=pl.ANY),) * 2,
        scratch_shapes=[pltpu.SemaphoreType.DMA((4,))],
        input_output_aliases={1: 0, 2: 1} if ends else {},
        compiler_params=pltpu.CompilerParams(vmem_limit_bytes=VMEM_LIMIT),
        name="place",
    )(data, *ends)


def call(kernel, shape, operands, space, scratch=(), name=None, flops=0, limit=VMEM_LIMIT, out_space=None):
    spec = pl.BlockSpec(memory_space=space)
    out_spec = pl.BlockSpec(memory_space=out_space or space)
    return pl.pallas_call(
        kernel,
        out_shape=jax.ShapeDtypeStruct(shape, jnp.bfloat16),
        in_specs=[spec] * len(operands),
        out_specs=out_spec,
        scratch_shapes=list(scratch),
        compiler_params=pltpu.CompilerParams(vmem_limit_bytes=limit),
        cost_estimate=pl.CostEstimate(
            flops=flops, bytes_accessed=4 * 1024 * 1024, transcendentals=0
        ),
        name=name,
    )(*operands)


def shards(psi_first, psi_second, left_env, right_env, links):
    tiles, width, _ = psi_first.shape
    terms, lefts, _, _ = left_env.shape
    rights = right_env.shape[1]
    peers = lax.axis_size(SEC)
    every = peers * tiles
    swap = [(0, 1), (1, 0)]

    upper = (rights + 1) // 2
    core = lax.axis_index("core")

    other_links = lax.ppermute(links, "v", swap)
    chosen_psi = jnp.where(lax.axis_index("v") == 0, psi_first, psi_second)
    pieces = chosen_psi.reshape(tiles, 2, width // 2, width).transpose(2, 0, 1, 3)
    pieces = pieces.reshape(peers * 2 * tiles, width)
    pieces = lax.all_to_all(pieces, SEC, split_axis=0, concat_axis=0, tiled=True)
    other_left = lax.ppermute(left_env, "v", swap)
    wanted = jnp.stack([links.reshape(peers, tiles), other_links.reshape(peers, tiles)], axis=1)
    hot = (wanted.reshape(2 * every, 1) == jnp.arange(every)[None, :]).astype(jnp.bfloat16)
    chosen = call(
        choose_kernel,
        (2 * every, 2 * width),
        (pieces, hot),
        pltpu.VMEM,
        scratch=[
            pltpu.VMEM((every, 2 * width), jnp.bfloat16),
            pltpu.VMEM((STEPS, 2 * every // STEPS, 2 * width), jnp.bfloat16),
            pltpu.SemaphoreType.DMA((STEPS,)),
        ],
        name="choose",
        out_space=pl.ANY,
        flops=700_000_000,
    )
    chosen, other_left = lax.optimization_barrier((chosen, other_left))
    arrived = lax.all_to_all(chosen, SEC, split_axis=0, concat_axis=0, tiled=True)
    near = lax.dynamic_slice_in_dim(right_env, core * (rights - upper), upper, 1)
    near = lax.ppermute(near, "v", swap)
    far = lax.ppermute(near, "core", swap)
    partial = call(
        apply_kernel,
        (tiles, width, width),
        (arrived, left_env, other_left, right_env, near, far),
        pltpu.VMEM,
        scratch=[
            pltpu.VMEM((2, lefts, width, rights * width), jnp.bfloat16),
            pltpu.VMEM((rights, lefts * width, 2 * terms * width), jnp.bfloat16),
        ],
        name="apply",
        flops=2_000_000_000,
    )
    quarters = lax.axis_size("q")
    axes = ("q", "v", "core")
    sets = [
        [(q * 2 + v) * 2 + c for q in (range(quarters) if c == 0 else reversed(range(quarters)))]
        for v in range(2)
        for c in range(2)
    ]
    parts = lax.all_to_all(
        partial, axes, split_axis=0, concat_axis=0, tiled=True, axis_index_groups=sets
    )
    parts = parts.reshape(quarters, tiles // quarters, width, width)
    mine = jnp.sum(parts.astype(jnp.float32), axis=0).astype(jnp.bfloat16)
    own = lax.all_gather(mine, axes, axis=0, tiled=True, axis_index_groups=sets)
    other = lax.ppermute(own, "v", swap)
    return place(1, other, *place(0, own))


def solution(mesh):
    ops, secs = mesh.devices.shape
    grid = Mesh(mesh.devices.reshape(ops // 2, 2, secs // 2, 2), ("q", "v", "chip", "core"))
    op, sec = ("q", "v"), SEC
    in_specs = (
        P(sec, None, None),
        P(sec, None, None),
        P(op, sec, None, None),
        P(op, None, None, None),
        P(op, None),
    )
    out_specs = (P(sec, None, None), P(sec, None, None))
    return jax.shard_map(shards, mesh=grid, in_specs=in_specs, out_specs=out_specs, check_vma=False)
```
